32 devices in a mesh: seq: 16 (over z, y, core), head: 2 (over x).
Axes of the slice: x: 2, y: 2, z: 4, core: 2. Of those that a mesh axis runs over, the one named last changes fastest.
Arguments:
- features: bfloat16 [16384, 1024], P('seq', 'head'), may hold values from -4.1875 to 4.1875
- cells: int32 [16384], P('seq'), may hold values from 0 to 16383, as said below
- conv7: bfloat16 [7, 7, 1024], P(None, None, 'head'), may hold values from -0.875 to 0.875
- conv5: bfloat16 [5, 5, 1024], P(None, None, 'head'), may hold values from -1.25 to 1.25
- conv3: bfloat16 [3, 3, 1024], P(None, None, 'head'), may hold values from -2 to 2
- conv_bias: bfloat16 [1024], P('head'), may hold values from -3 to 3
- w_qkv: bfloat16 [1024, 3, 1024], P(None, None, 'head'), may hold values from -5 to 5
Outputs:
- attended: bfloat16 [16384, 1024], P('seq', 'head')
The draws below stay inside these ranges and needn't reach their ends.
Inputs may be any that keep to these rules, and one draw needn't show every extreme that they name: cells names each of the 16384 grid cells once. Of the 1024 entries held by one index of seq, at most 128 lie in any one band of 1024 consecutive cells, and exactly 128 lie in some band; every band receives exactly 128 from some index of seq.
All inputs are finite; a program needn't handle non-finite values.
Results may differ from the reference program's by a relative error of at most 0.0052.
Values may be sent and summed in bfloat16 or wider, within the bound.
A program may use at most 128 MiB of HBM per device.

```python
import math
import jax
import jax.numpy as jnp
from jax import lax

D = 1024
HEADS = 16
HEAD_DIM = 64
GRID_W = 256
TOK_DEV = 1024
ROWS = 64
TOKENS = 16384
N_SEQ = 16


def draw_cells(key, part):
    members = TOKENS // TOK_DEV
    half_load = TOK_DEV // members
    first, second, third, fourth = jax.random.split(key, 4)
    spread = jax.random.randint(first, (members // 2,), 0, half_load + 1).astype(jnp.int32)
    spread = spread.at[0].set(half_load)
    shift_loads = jnp.stack([half_load + spread, half_load - spread], axis=1).reshape(members)
    shift_order = jax.random.permutation(second, members)
    shift_loads = shift_loads[shift_order]
    seg_ends = jnp.cumsum(shift_loads)
    slot_index = jnp.arange(TOK_DEV, dtype=jnp.int32)
    shift_of = jnp.sum((seg_ends[None, :] <= slot_index[:, None]).astype(jnp.int32), axis=1)
    band_perms = jax.vmap(lambda sub_key: jax.random.permutation(sub_key, TOK_DEV))(jax.random.split(third, members)).astype(jnp.int32)
    source = jnp.arange(members, dtype=jnp.int32)
    band_of = (source[:, None] - shift_of[None, :] + members) % members
    cell_ids = band_of * TOK_DEV + band_perms[band_of, slot_index[None, :]]
    scramble = jax.vmap(lambda sub_key: jax.random.permutation(sub_key, TOK_DEV))(jax.random.split(fourth, members)).astype(jnp.int32)
    cell_ids = jnp.take_along_axis(cell_ids, scramble, axis=1)
    return cell_ids.reshape(TOKENS).astype(jnp.int32)


def draw_w_qkv(key, part):
    noise = jax.random.normal(key, (D, 3, D), jnp.float32) * (1.0 / math.sqrt(D))
    return noise.astype(jnp.bfloat16)


def block_levels(stream_key, extent, shards, low, high):
    gain = 1.0
    for position, parts in shards:
        draws = jax.random.uniform(jax.random.fold_in(jax.random.fold_in(stream_key, 6), position), (parts,), jnp.float32, low / len(shards), high / len(shards))
        gain = gain * jnp.repeat(jnp.exp(draws), extent[position] // parts).reshape((-1,) + (1,) * (len(extent) - 1 - position))
    return gain


def gaussian(rng, shape, scale, limit, shards=(), held_as=jnp.bfloat16):
    values = jax.random.normal(rng, shape, jnp.float32) * scale
    if len(shards) > 0:
        values = block_levels(rng, shape, shards, -0.22, 0.18) * values
    return jnp.clip(values, min=-limit, max=limit).astype(held_as)


def setup_inputs(seed: int = 0) -> dict:
    streams_of = jax.random.split(jax.random.key(seed), 8)
    features = gaussian(streams_of[0], (TOKENS, D), 0.7, 4.1875, ((0, 16), (1, 2)))
    cells = draw_cells(jax.random.fold_in(streams_of[7], 71), 0)
    conv7 = gaussian(streams_of[2], (7, 7, D), 49 ** -0.5, 0.875, ((2, 2),))
    conv5 = gaussian(streams_of[3], (5, 5, D), 25 ** -0.5, 1.25, ((2, 2),))
    conv3 = gaussian(streams_of[4], (3, 3, D), 9 ** -0.5, 2.0, ((2, 2),))
    conv_bias = gaussian(streams_of[5], (D,), 0.5, 3.0, ((0, 2),))
    w_qkv = draw_w_qkv(jax.random.fold_in(streams_of[7], 71), 0)
    return {"features": features, "cells": cells, "conv7": conv7, "conv5": conv5, "conv3": conv3, "conv_bias": conv_bias, "w_qkv": w_qkv}


def depthwise(padded, kernel, margin, height, width):
    reach = kernel.shape[0]
    result = jnp.zeros((height, width, padded.shape[2]), jnp.float32)
    for i in range(reach):
        for j in range(reach):
            result = result + padded[margin + i:margin + i + height, margin + j:margin + j + width] * kernel[i, j].astype(jnp.float32)
    return result

def reference(features, cells, conv7, conv5, conv3, conv_bias, w_qkv):
    placed = jnp.zeros((TOKENS, D), jnp.bfloat16).at[cells].set(features)
    grid_cells = placed.reshape(ROWS, GRID_W, D).astype(jnp.float32)
    padded = jnp.pad(grid_cells, ((3, 3), (3, 3), (0, 0)))
    mixed_sum = grid_cells + conv_bias.astype(jnp.float32)
    for kernel in (conv7, conv5, conv3):
        mixed_sum = mixed_sum + depthwise(padded, kernel, 3 - kernel.shape[0] // 2, ROWS, GRID_W)
    ppeg = mixed_sum.astype(jnp.bfloat16).reshape(TOKENS, D)
    projected = jnp.dot(ppeg, w_qkv.reshape(D, 3 * D), preferred_element_type=jnp.float32).astype(jnp.bfloat16)
    queries = projected[:, :D].reshape(TOKENS, HEADS, HEAD_DIM)
    key_rows = projected[:, D:2 * D].reshape(TOKENS, HEADS, HEAD_DIM)
    value_rows = projected[:, 2 * D:].reshape(TOKENS, HEADS, HEAD_DIM)
    score_scale = 1.0 / math.sqrt(HEAD_DIM)

    def attend(band_index):
        start = (band_index * TOK_DEV).astype(jnp.int32)
        before = ((band_index + N_SEQ - 1) % N_SEQ * TOK_DEV).astype(jnp.int32)
        query_band = lax.dynamic_slice_in_dim(queries, start, TOK_DEV, 0).astype(jnp.float32)
        key_band = jnp.concatenate([lax.dynamic_slice_in_dim(key_rows, start, TOK_DEV, 0), lax.dynamic_slice_in_dim(key_rows, before, TOK_DEV, 0)], axis=0).astype(jnp.float32)
        value_band = jnp.concatenate([lax.dynamic_slice_in_dim(value_rows, start, TOK_DEV, 0), lax.dynamic_slice_in_dim(value_rows, before, TOK_DEV, 0)], axis=0).astype(jnp.float32)
        scores = jnp.einsum('thd,uhd->thu', query_band, key_band) * score_scale
        row_top = lax.optimization_barrier(jnp.max(scores, axis=2, keepdims=True))
        weight = jnp.exp(scores - row_top)
        weight_sum = lax.optimization_barrier(jnp.sum(weight, axis=2))
        probs = lax.optimization_barrier(weight.astype(jnp.bfloat16)).astype(jnp.float32)
        summed = jnp.einsum('thu,uhd->thd', probs, value_band)
        return (summed / weight_sum[:, :, None]).astype(jnp.bfloat16).reshape(TOK_DEV, D)
    attended = lax.map(attend, jnp.arange(N_SEQ, dtype=jnp.int32))
    return attended.reshape(TOKENS, D)
```

```python
import functools
import math

import jax
import jax.numpy as jnp
from jax import lax
from jax.experimental import pallas as pl
from jax.experimental.pallas import tpu as pltpu
from jax.sharding import PartitionSpec as P

D = 1024
HEADS = 16
GRID_W = 256
LANES = 128
PAD = 8
STRIP = 64
REACH = 7
HALO = REACH // 2
QUERY_ROWS = 256
MESH = pl.DeviceIdType.MESH
VMEM_BYTES = 56 * 1024 * 1024


def iota(shape, dim):
    return lax.broadcasted_iota(jnp.int32, shape, dim)


def flags(condition):
    return jnp.where(condition, 1.0, 0.0)


def route_kernel(members, capacity, owner_ref, within_ref, features_ref, out_ref, places_ref):
    tok_dev, local_dim = features_ref.shape
    owner = owner_ref[...]
    onehot = flags(iota((members, tok_dev), 0) == owner)
    upper = flags(iota((tok_dev, tok_dev), 0) < iota((tok_dev, tok_dev), 1))
    earlier = jnp.dot(
        onehot.astype(jnp.bfloat16),
        upper.astype(jnp.bfloat16),
        preferred_element_type=jnp.float32,
    )
    rank = jnp.sum(earlier * onehot, axis=0, keepdims=True)
    slot = owner * capacity + rank.astype(jnp.int32)
    within = within_ref[...]
    line = iota((8, tok_dev), 0)
    high = (within >> 8).astype(jnp.float32)
    low = (within & 255).astype(jnp.float32)
    code = jnp.where(line == 0, high, jnp.where(line == 1, low, jnp.where(line == 2, 1.0, 0.0)))
    code = code.astype(jnp.bfloat16)

    def to_band(band, carry):
        pick = flags(iota((capacity, tok_dev), 0) + band * capacity == slot).astype(jnp.bfloat16)
        rows = jnp.dot(pick, features_ref[...], preferred_element_type=jnp.float32)
        rows = rows.astype(jnp.bfloat16)
        for chunk in range(local_dim // LANES):
            out_ref[chunk, band] = rows[:, chunk * LANES : (chunk + 1) * LANES]
        found = lax.dot_general(
            code, pick, (((1,), (1,)), ((), ())), preferred_element_type=jnp.float32
        )
        place = jnp.where(found[2:3] > 0.5, found[0:1] * 256.0 + found[1:2], -1.0)
        places_ref[band] = jnp.broadcast_to(place.astype(jnp.int32), (8, capacity))
        return carry

    lax.fori_loop(0, members, to_band, 0)


def mix_kernel(
    members,
    outgoing_ref,
    places_ref,
    taps_ref,
    bias_ref,
    mixed_ref,
    arrived,
    places_in,
    gather,
    band_bf16,
    halo_up,
    halo_down,
    padded,
    own,
    other,
    out_send,
    out_recv,
    place_send,
    place_recv,
    up_send,
    up_recv,
    down_send,
    down_recv,
    pair_send,
    pair_recv,
):
    chunks, _, capacity, _ = outgoing_ref.shape
    tok_dev = mixed_ref.shape[0]
    local_dim = mixed_ref.shape[1] // 2
    band_rows = tok_dev // GRID_W
    halo_len = HALO * GRID_W
    me = lax.axis_index("seq")
    half = lax.axis_index("head")

    barrier = pltpu.get_barrier_semaphore()

    def greet(step, carry):
        peer = lax.rem(me + step, members)
        pl.semaphore_signal(barrier, inc=1, device_id={"seq": peer}, device_id_type=MESH)
        return carry

    lax.fori_loop(1, members, greet, 0)
    pl.semaphore_signal(barrier, inc=1, device_id={"head": 1 - half}, device_id_type=MESH)
    pl.semaphore_wait(barrier, members)

    def place_copy(peer, slot):
        return pltpu.make_async_remote_copy(
            src_ref=places_ref.at[peer],
            dst_ref=places_in.at[slot],
            send_sem=place_send.at[peer],
            recv_sem=place_recv.at[slot],
            device_id={"seq": peer},
            device_id_type=MESH,
        )

    def token_copy(chunk, peer, slot):
        return pltpu.make_async_remote_copy(
            src_ref=outgoing_ref.at[chunk, peer],
            dst_ref=arrived.at[chunk, slot],
            send_sem=out_send.at[chunk, peer],
            recv_sem=out_recv.at[chunk, slot],
            device_id={"seq": peer},
            device_id_type=MESH,
        )

    def each_peer(action):
        def step_body(step, carry):
            action(lax.rem(me + step, members))
            return carry

        lax.fori_loop(1, members, step_body, 0)

    each_peer(lambda peer: place_copy(peer, me).start())
    for chunk in range(min(2, chunks)):
        each_peer(lambda peer: token_copy(chunk, peer, me).start())

    places_in[pl.ds(me, 1)] = places_ref[pl.ds(me, 1)]
    for chunk in range(chunks):
        arrived[chunk, pl.ds(me, 1)] = outgoing_ref[chunk, pl.ds(me, 1)]
    edge = jnp.zeros((band_rows + 2 * HALO, PAD, LANES), jnp.float32)
    padded[:, 0:PAD, :] = edge
    padded[:, PAD + GRID_W :, :] = edge

    each_peer(lambda peer: place_copy(peer, peer).wait_recv())

    def pick_rows(row, carry):
        start = pl.multiple_of(row * GRID_W, GRID_W)
        cell = iota((GRID_W, capacity), 0) + start
        for source in range(members):
            hit = flags(cell == places_in[source, 0:1, :])
            gather[pl.ds(start, GRID_W), source * capacity : (source + 1) * capacity] = hit.astype(
                jnp.bfloat16
            )
        return carry

    lax.fori_loop(0, band_rows, pick_rows, 0)

    above = lax.rem(me + members - 1, members)
    below = lax.rem(me + 1, members)

    def copy_up(chunk):
        return pltpu.make_async_remote_copy(
            src_ref=band_bf16.at[chunk, pl.ds(0, halo_len)],
            dst_ref=halo_down.at[chunk],
            send_sem=up_send.at[chunk],
            recv_sem=up_recv.at[chunk],
            device_id={"seq": above},
            device_id_type=MESH,
        )

    def copy_down(chunk):
        return pltpu.make_async_remote_copy(
            src_ref=band_bf16.at[chunk, pl.ds(tok_dev - halo_len, halo_len)],
            dst_ref=halo_up.at[chunk],
            send_sem=down_send.at[chunk],
            recv_sem=down_recv.at[chunk],
            device_id={"seq": below},
            device_id_type=MESH,
        )

    def pair_copy(chunk):
        return pltpu.make_async_remote_copy(
            src_ref=own.at[chunk],
            dst_ref=other.at[chunk],
            send_sem=pair_send.at[chunk],
            recv_sem=pair_recv.at[chunk],
            device_id={"head": 1 - half},
            device_id_type=MESH,
        )

    has_above = me > 0
    has_below = me < members - 1

    def place(chunk):
        each_peer(lambda peer: token_copy(chunk, peer, peer).wait_recv())
        tokens = arrived[chunk].reshape(members * capacity, LANES)
        for row in range(band_rows):
            cells = slice(row * GRID_W, (row + 1) * GRID_W)
            found = jnp.dot(gather[cells, :], tokens, preferred_element_type=jnp.float32)
            band_bf16[chunk, cells, :] = found.astype(jnp.bfloat16)

        @pl.when(has_above)
        def _():
            copy_up(chunk).start()

        @pl.when(has_below)
        def _():
            copy_down(chunk).start()

        if chunk + 2 < chunks:
            each_peer(lambda peer: token_copy(chunk, peer, me).wait_send())
            each_peer(lambda peer: token_copy(chunk + 2, peer, me).start())

    def convolve(chunk):
        for row in range(band_rows):
            padded[HALO + row, PAD : PAD + GRID_W, :] = band_bf16[
                chunk, row * GRID_W : (row + 1) * GRID_W, :
            ].astype(jnp.float32)

        blank = jnp.zeros((HALO, GRID_W, LANES), jnp.float32)

        @pl.when(has_above)
        def _():
            copy_down(chunk).wait_recv()
            for row in range(HALO):
                padded[row, PAD : PAD + GRID_W, :] = halo_up[
                    chunk, row * GRID_W : (row + 1) * GRID_W, :
                ].astype(jnp.float32)

        @pl.when(jnp.logical_not(has_above))
        def _():
            padded[0:HALO, PAD : PAD + GRID_W, :] = blank

        @pl.when(has_below)
        def _():
            copy_up(chunk).wait_recv()
            for row in range(HALO):
                padded[HALO + band_rows + row, PAD : PAD + GRID_W, :] = halo_down[
                    chunk, row * GRID_W : (row + 1) * GRID_W, :
                ].astype(jnp.float32)

        @pl.when(jnp.logical_not(has_below))
        def _():
            padded[HALO + band_rows :, PAD : PAD + GRID_W, :] = blank

        lanes = slice(chunk * LANES, (chunk + 1) * LANES)
        columns = pl.ds(pl.multiple_of(half * local_dim + chunk * LANES, LANES), LANES)

        def strip(index, carry):
            start = pl.multiple_of(index * STRIP, STRIP)
            sums = [jnp.broadcast_to(bias_ref[:, lanes], (STRIP, LANES))] * band_rows
            for j in range(REACH):
                for line in range(band_rows + 2 * HALO):
                    cells = padded[line, pl.ds(start + (PAD - HALO + j), STRIP), :]
                    for row in range(max(0, line - 2 * HALO), min(band_rows, line + 1)):
                        tap = (line - row) * REACH + j
                        sums[row] = sums[row] + cells * taps_ref[tap : tap + 1, lanes]
            for row in range(band_rows):
                value = sums[row].astype(jnp.bfloat16)
                where = pl.ds(pl.multiple_of(row * GRID_W + start, STRIP), STRIP)
                own[chunk, where, :] = value
                mixed_ref[where, columns] = value
            return carry

        lax.fori_loop(0, GRID_W // STRIP, strip, 0)
        pair_copy(chunk).start()

    for chunk in range(chunks + 1):
        if chunk < chunks:
            place(chunk)
        if chunk > 0:
            convolve(chunk - 1)

    for chunk in range(chunks):
        pair_copy(chunk).wait_recv()
        columns = pl.ds(pl.multiple_of((1 - half) * local_dim + chunk * LANES, LANES), LANES)
        mixed_ref[:, columns] = other[chunk]

    each_peer(lambda peer: place_copy(peer, me).wait_send())
    for chunk in range(chunks):
        pair_copy(chunk).wait_send()
        if chunk + 2 >= chunks:
            each_peer(lambda peer: token_copy(chunk, peer, me).wait_send())

        @pl.when(has_above)
        def _():
            copy_up(chunk).wait_send()

        @pl.when(has_below)
        def _():
            copy_down(chunk).wait_send()


def attend_kernel(
    members, head_dim, mixed_ref, weights_ref, out_ref, queries, kept, prior, top, numer, denom, send, recv
):
    tok_dev = mixed_ref.shape[0]
    local_dim = weights_ref.shape[1] // 3
    chunks = local_dim // LANES
    me = lax.axis_index("seq")
    above = lax.rem(me + members - 1, members)
    below = lax.rem(me + 1, members)
    scale = 1.0 / math.sqrt(head_dim)

    barrier = pltpu.get_barrier_semaphore()
    for neighbour in (above, below):
        pl.semaphore_signal(barrier, inc=1, device_id={"seq": neighbour}, device_id_type=MESH)
    pl.semaphore_wait(barrier, 2)

    def band_copy(chunk):
        return pltpu.make_async_remote_copy(
            src_ref=kept.at[chunk],
            dst_ref=prior.at[chunk],
            send_sem=send.at[chunk],
            recv_sem=recv.at[chunk],
            device_id={"seq": below},
            device_id_type=MESH,
        )

    blocks = tok_dev // QUERY_ROWS

    for chunk in range(chunks):
        for kind in range(2):
            first = (kind + 1) * local_dim + chunk * LANES
            part = weights_ref[:, first : first + LANES]

            def project(index, carry):
                rows = pl.ds(pl.multiple_of(index * QUERY_ROWS, QUERY_ROWS), QUERY_ROWS)
                kept[chunk, kind, rows, :] = jnp.dot(
                    mixed_ref[rows, :], part, preferred_element_type=jnp.float32
                ).astype(jnp.bfloat16)
                return carry

            lax.fori_loop(0, blocks, project, 0)
        band_copy(chunk).start()

    def project_queries(index, carry):
        rows = pl.ds(pl.multiple_of(index * QUERY_ROWS, QUERY_ROWS), QUERY_ROWS)
        product = jnp.dot(
            mixed_ref[rows, :], weights_ref[:, :local_dim], preferred_element_type=jnp.float32
        ).astype(jnp.bfloat16)
        for chunk in range(chunks):
            queries[chunk, rows, :] = product[:, chunk * LANES : (chunk + 1) * LANES] * jnp.asarray(
                scale, jnp.bfloat16
            )
        return carry

    lax.fori_loop(0, blocks, project_queries, 0)

    def partial(chunk, block_rows, source):
        query = queries[chunk, block_rows, :]
        lane_q = iota(query.shape, 1)
        keys = source[chunk, 0]
        values = source[chunk, 1]
        lane_v = iota(values.shape, 1)
        peak = total = summed = None
        for head in range(LANES // head_dim):
            mine_q = lane_q // head_dim == head
            mine_v = lane_v // head_dim == head
            score = lax.dot_general(
                jnp.where(mine_q, query, jnp.zeros_like(query)),
                keys,
                (((1,), (1,)), ((), ())),
                preferred_element_type=jnp.float32,
            )
            high = jnp.max(score, axis=1, keepdims=True)
            probs = jnp.exp(score - high).astype(jnp.bfloat16)
            both = jnp.dot(
                probs,
                jnp.where(mine_v, values, jnp.ones_like(values)),
                preferred_element_type=jnp.float32,
            )
            swapped = pltpu.roll(both, head_dim, 1)
            high = jnp.broadcast_to(high, both.shape)
            if head == 0:
                peak, total, summed = high, swapped, both
            else:
                peak = jnp.where(mine_q, high, peak)
                total = jnp.where(mine_q, swapped, total)
                summed = jnp.where(mine_q, both, summed)
        return peak, total, summed

    for chunk in range(chunks):

        def attend_own(index, carry):
            rows = pl.ds(pl.multiple_of(index * QUERY_ROWS, QUERY_ROWS), QUERY_ROWS)
            peak, total, summed = partial(chunk, rows, kept)
            top[chunk, rows, :] = peak
            denom[chunk, rows, :] = total
            numer[chunk, rows, :] = summed
            return carry

        lax.fori_loop(0, blocks, attend_own, 0)

    for chunk in range(chunks):
        band_copy(chunk).wait_recv()

        def attend_prior(index, carry):
            rows = pl.ds(pl.multiple_of(index * QUERY_ROWS, QUERY_ROWS), QUERY_ROWS)
            peak, total, summed = partial(chunk, rows, prior)
            before = top[chunk, rows, :]
            high = jnp.maximum(peak, before)
            here = jnp.exp(peak - high)
            there = jnp.exp(before - high)
            total = total * here + denom[chunk, rows, :] * there
            summed = summed * here + numer[chunk, rows, :] * there
            out_ref[rows, chunk * LANES : (chunk + 1) * LANES] = (summed / total).astype(jnp.bfloat16)
            return carry

        lax.fori_loop(0, blocks, attend_prior, 0)

    for chunk in range(chunks):
        band_copy(chunk).wait_send()


def shards(features, cells, conv7, conv5, conv3, conv_bias, w_qkv):
    tok_dev, local_dim = features.shape
    members = lax.axis_size("seq")
    capacity = 2 * tok_dev // members
    chunks = local_dim // LANES
    head_dim = D // HEADS
    band_rows = tok_dev // GRID_W
    halo_len = HALO * GRID_W
    vmem = pl.BlockSpec(memory_space=pltpu.VMEM)
    dma = pltpu.SemaphoreType.DMA

    owner = (cells // tok_dev).reshape(1, tok_dev)
    within = cells.reshape(1, tok_dev) - owner * tok_dev
    outgoing, places = pl.pallas_call(
        functools.partial(route_kernel, members, capacity),
        out_shape=(
            jax.ShapeDtypeStruct((chunks, members, capacity, LANES), jnp.bfloat16),
            jax.ShapeDtypeStruct((members, 8, capacity), jnp.int32),
        ),
        in_specs=[vmem] * 3,
        out_specs=(vmem, vmem),
        compiler_params=pltpu.CompilerParams(vmem_limit_bytes=VMEM_BYTES),
        name="route",
    )(owner, within, features)

    merged = conv7.astype(jnp.float32) + jnp.pad(
        conv5.astype(jnp.float32), ((1, 1), (1, 1), (0, 0))
    )
    merged = merged + jnp.pad(conv3.astype(jnp.float32), ((2, 2), (2, 2), (0, 0)))
    merged = merged + jnp.pad(jnp.ones((1, 1, local_dim), jnp.float32), ((3, 3), (3, 3), (0, 0)))
    taps = merged.reshape(REACH * REACH, local_dim)
    bias = conv_bias.astype(jnp.float32).reshape(1, local_dim)

    mixed = pl.pallas_call(
        functools.partial(mix_kernel, members),
        out_shape=jax.ShapeDtypeStruct((tok_dev, 2 * local_dim), jnp.bfloat16),
        in_specs=[vmem] * 4,
        out_specs=vmem,
        scratch_shapes=[
            pltpu.VMEM((chunks, members, capacity, LANES), jnp.bfloat16),
            pltpu.VMEM((members, 8, capacity), jnp.int32),
            pltpu.VMEM((tok_dev, members * capacity), jnp.bfloat16),
            pltpu.VMEM((chunks, tok_dev, LANES), jnp.bfloat16),
            pltpu.VMEM((chunks, halo_len, LANES), jnp.bfloat16),
            pltpu.VMEM((chunks, halo_len, LANES), jnp.bfloat16),
            pltpu.VMEM((band_rows + 2 * HALO, GRID_W + 2 * PAD, LANES), jnp.float32),
            pltpu.VMEM((chunks, tok_dev, LANES), jnp.bfloat16),
            pltpu.VMEM((chunks, tok_dev, LANES), jnp.bfloat16),
            dma((chunks, members)),
            dma((chunks, members)),
            dma((members,)),
            dma((members,)),
            dma((chunks,)),
            dma((chunks,)),
            dma((chunks,)),
            dma((chunks,)),
            dma((chunks,)),
            dma((chunks,)),
        ],
        compiler_params=pltpu.CompilerParams(
            collective_id=0, has_side_effects=True, vmem_limit_bytes=VMEM_BYTES
        ),
        name="mix",
    )(outgoing, places, taps, bias)

    weights = w_qkv.reshape(w_qkv.shape[0], 3 * local_dim)
    return pl.pallas_call(
        functools.partial(attend_kernel, members, head_dim),
        out_shape=jax.ShapeDtypeStruct((tok_dev, local_dim), jnp.bfloat16),
        in_specs=[vmem] * 2,
        out_specs=vmem,
        scratch_shapes=[
            pltpu.VMEM((chunks, tok_dev, LANES), jnp.bfloat16),
            pltpu.VMEM((chunks, 2, tok_dev, LANES), jnp.bfloat16),
            pltpu.VMEM((chunks, 2, tok_dev, LANES), jnp.bfloat16),
            pltpu.VMEM((chunks, tok_dev, LANES), jnp.float32),
            pltpu.VMEM((chunks, tok_dev, LANES), jnp.float32),
            pltpu.VMEM((chunks, tok_dev, LANES), jnp.float32),
            dma((chunks,)),
            dma((chunks,)),
        ],
        compiler_params=pltpu.CompilerParams(
            collective_id=1, has_side_effects=True, vmem_limit_bytes=VMEM_BYTES
        ),
        name="attend",
    )(mixed, weights)


def solution(mesh):
    placed = (
        P("seq", "head"),
        P("seq"),
        P(None, None, "head"),
        P(None, None, "head"),
        P(None, None, "head"),
        P("head"),
        P(None, None, "head"),
    )
    return jax.shard_map(
        shards, mesh=mesh, in_specs=placed, out_specs=P("seq", "head"), check_vma=False
    )
```

```python
import functools
import math

import jax
import jax.numpy as jnp
from jax import lax
from jax.experimental import pallas as pl
from jax.experimental.pallas import tpu as pltpu
from jax.sharding import PartitionSpec as P

D = 1024
HEADS = 16
GRID_W = 256
LANES = 128
PAD = 8
STRIP = 32
REACH = 7
HALO = REACH // 2
QUERY_ROWS = 512
MESH = pl.DeviceIdType.MESH
VMEM_BYTES = 56 * 1024 * 1024


def iota(shape, dim):
    return lax.broadcasted_iota(jnp.int32, shape, dim)


def flags(condition):
    return jnp.where(condition, 1.0, 0.0)


def band_kernel(
    members,
    head_dim,
    cells_ref,
    features_ref,
    weights_hbm,
    taps_ref,
    bias_ref,
    out_ref,
    outgoing_ref,
    places_ref,
    mixed_ref,
    arrived,
    places_in,
    gather,
    band_bf16,
    halo_up,
    halo_down,
    padded,
    weights_ref,
    queries,
    keys_own,
    values_own,
    keys_prior,
    values_prior,
    top,
    numer,
    denom,
    weight_sem,
    out_send,
    out_recv,
    place_send,
    place_recv,
    up_send,
    up_recv,
    down_send,
    down_recv,
    pair_send,
    pair_recv,
    key_send,
    key_recv,
    value_send,
    value_recv,
):
    chunks, _, capacity, _ = outgoing_ref.shape
    fetch = pltpu.make_async_copy(weights_hbm, weights_ref, weight_sem)
    fetch.start()
    tok_dev, local_dim = out_ref.shape
    band_rows = tok_dev // GRID_W
    halo_len = HALO * GRID_W
    me = lax.axis_index("seq")
    half = lax.axis_index("head")

    barrier = pltpu.get_barrier_semaphore()

    def greet(step, carry):
        peer = lax.rem(me + step, members)
        pl.semaphore_signal(barrier, inc=1, device_id={"seq": peer}, device_id_type=MESH)
        return carry

    lax.fori_loop(1, members, greet, 0)
    pl.semaphore_signal(barrier, inc=1, device_id={"head": 1 - half}, device_id_type=MESH)
    pl.semaphore_wait(barrier, members)

    def place_copy(peer, slot):
        return pltpu.make_async_remote_copy(
            src_ref=places_ref.at[peer],
            dst_ref=places_in.at[slot],
            send_sem=place_send.at[peer],
            recv_sem=place_recv.at[slot],
            device_id={"seq": peer},
            device_id_type=MESH,
        )

    def token_copy(chunk, peer, slot):
        return pltpu.make_async_remote_copy(
            src_ref=outgoing_ref.at[chunk, peer],
            dst_ref=arrived.at[chunk, slot],
            send_sem=out_send.at[chunk, peer],
            recv_sem=out_recv.at[chunk, slot],
            device_id={"seq": peer},
            device_id_type=MESH,
        )

    def each_peer(action):
        def step_body(step, carry):
            away = (step + 1) // 2
            shift = members // 2 + lax.select(lax.rem(step, 2) == 1, away, -away)
            action(lax.rem(me + shift, members))
            return carry

        lax.fori_loop(0, members - 1, step_body, 0)

    cells = cells_ref[...]
    owner = ((cells.astype(jnp.float32) + 0.5) * (1.0 / tok_dev)).astype(jnp.int32)
    within = cells - owner * tok_dev
    onehot = flags(iota((members, tok_dev), 0) == owner)
    upper = flags(iota((tok_dev, tok_dev), 0) < iota((tok_dev, tok_dev), 1))
    earlier = jnp.dot(
        onehot.astype(jnp.bfloat16),
        upper.astype(jnp.bfloat16),
        preferred_element_type=jnp.float32,
    )
    rank = jnp.sum(earlier * onehot, axis=0, keepdims=True)
    slot = owner * capacity + rank.astype(jnp.int32)
    line = iota((8, tok_dev), 0)
    high = (within >> 8).astype(jnp.float32)
    low = (within & 255).astype(jnp.float32)
    code = jnp.where(line == 0, high, jnp.where(line == 1, low, jnp.where(line == 2, 1.0, 0.0)))
    code = code.astype(jnp.bfloat16)

    def pack(band):
        pick = flags(iota((capacity, tok_dev), 0) + band * capacity == slot).astype(jnp.bfloat16)
        rows = jnp.dot(pick, features_ref[...], preferred_element_type=jnp.float32)
        rows = rows.astype(jnp.bfloat16)
        for chunk in range(chunks):
            outgoing_ref[chunk, band] = rows[:, chunk * LANES : (chunk + 1) * LANES]
        found = lax.dot_general(
            code, pick, (((1,), (1,)), ((), ())), preferred_element_type=jnp.float32
        )
        spot = jnp.where(found[2:3] > 0.5, found[0:1] * 256.0 + found[1:2], -1.0)
        places_ref[band] = jnp.broadcast_to(spot.astype(jnp.int32), (8, capacity))

    def pack_and_send(peer):
        pack(peer)
        place_copy(peer, me).start()
        token_copy(0, peer, me).start()

    each_peer(pack_and_send)
    if chunks > 1:
        each_peer(lambda peer: token_copy(1, peer, me).start())
    pack(me)

    places_in[pl.ds(me, 1)] = places_ref[pl.ds(me, 1)]
    for chunk in range(chunks):
        arrived[chunk, pl.ds(me, 1)] = outgoing_ref[chunk, pl.ds(me, 1)]
    edge = jnp.zeros((band_rows + 2 * HALO, PAD, LANES), jnp.float32)
    padded[:, 0:PAD, :] = edge
    padded[:, PAD + GRID_W :, :] = edge

    each_peer(lambda peer: place_copy(peer, peer).wait_recv())

    def pick_rows(row, carry):
        start = pl.multiple_of(row * GRID_W, GRID_W)
        cell = iota((GRID_W, capacity), 0) + start
        for source in range(members):
            hit = flags(cell == places_in[source, 0:1, :])
            gather[pl.ds(start, GRID_W), source * capacity : (source + 1) * capacity] = hit.astype(
                jnp.bfloat16
            )
        return carry

    lax.fori_loop(0, band_rows, pick_rows, 0)

    above = lax.rem(me + members - 1, members)
    below = lax.rem(me + 1, members)

    def copy_up(chunk):
        return pltpu.make_async_remote_copy(
            src_ref=band_bf16.at[chunk, pl.ds(0, halo_len)],
            dst_ref=halo_down.at[chunk],
            send_sem=up_send.at[chunk],
            recv_sem=up_recv.at[chunk],
            device_id={"seq": above},
            device_id_type=MESH,
        )

    def copy_down(chunk):
        return pltpu.make_async_remote_copy(
            src_ref=band_bf16.at[chunk, pl.ds(tok_dev - halo_len, halo_len)],
            dst_ref=halo_up.at[chunk],
            send_sem=down_send.at[chunk],
            recv_sem=down_recv.at[chunk],
            device_id={"seq": below},
            device_id_type=MESH,
        )

    def own_columns(chunk):
        return pl.ds(pl.multiple_of(half * local_dim + chunk * LANES, LANES), LANES)

    def pair_copy(chunk):
        return pltpu.make_async_remote_copy(
            src_ref=mixed_ref.at[:, own_columns(chunk)],
            dst_ref=mixed_ref.at[:, own_columns(chunk)],
            send_sem=pair_send.at[chunk],
            recv_sem=pair_recv.at[chunk],
            device_id={"head": 1 - half},
            device_id_type=MESH,
        )

    has_above = me > 0
    has_below = me < members - 1

    def place(chunk):
        each_peer(lambda peer: token_copy(chunk, peer, peer).wait_recv())
        tokens = arrived[chunk].reshape(members * capacity, LANES)
        for row in range(band_rows):
            cells = slice(row * GRID_W, (row + 1) * GRID_W)
            found = jnp.dot(gather[cells, :], tokens, preferred_element_type=jnp.float32)
            band_bf16[chunk, cells, :] = found.astype(jnp.bfloat16)

        @pl.when(has_above)
        def _():
            copy_up(chunk).start()

        @pl.when(has_below)
        def _():
            copy_down(chunk).start()

        if chunk + 2 < chunks:
            each_peer(lambda peer: token_copy(chunk, peer, me).wait_send())
            each_peer(lambda peer: token_copy(chunk + 2, peer, me).start())

    def convolve(chunk):
        for row in range(band_rows):
            padded[HALO + row, PAD : PAD + GRID_W, :] = band_bf16[
                chunk, row * GRID_W : (row + 1) * GRID_W, :
            ].astype(jnp.float32)

        blank = jnp.zeros((HALO, GRID_W, LANES), jnp.float32)

        @pl.when(has_above)
        def _():
            copy_down(chunk).wait_recv()
            for row in range(HALO):
                padded[row, PAD : PAD + GRID_W, :] = halo_up[
                    chunk, row * GRID_W : (row + 1) * GRID_W, :
                ].astype(jnp.float32)

        @pl.when(jnp.logical_not(has_above))
        def _():
            padded[0:HALO, PAD : PAD + GRID_W, :] = blank

        @pl.when(has_below)
        def _():
            copy_up(chunk).wait_recv()
            for row in range(HALO):
                padded[HALO + band_rows + row, PAD : PAD + GRID_W, :] = halo_down[
                    chunk, row * GRID_W : (row + 1) * GRID_W, :
                ].astype(jnp.float32)

        @pl.when(jnp.logical_not(has_below))
        def _():
            padded[HALO + band_rows :, PAD : PAD + GRID_W, :] = blank

        lanes = slice(chunk * LANES, (chunk + 1) * LANES)
        columns = own_columns(chunk)

        def strip(index, carry):
            start = pl.multiple_of(index * STRIP, STRIP)
            sums = [jnp.broadcast_to(bias_ref[:, lanes], (STRIP, LANES))] * band_rows
            for j in range(REACH):
                taps = [taps_ref[i * REACH + j : i * REACH + j + 1, lanes] for i in range(REACH)]
                for line in range(band_rows + 2 * HALO):
                    cells = padded[line, pl.ds(start + (PAD - HALO + j), STRIP), :]
                    for row in range(max(0, line - 2 * HALO), min(band_rows, line + 1)):
                        sums[row] = sums[row] + cells * taps[line - row]
            for row in range(band_rows):
                value = sums[row].astype(jnp.bfloat16)
                where = pl.ds(pl.multiple_of(row * GRID_W + start, STRIP), STRIP)
                mixed_ref[where, columns] = value
            return carry

        lax.fori_loop(0, GRID_W // STRIP, strip, 0)
        pair_copy(chunk).start()

    for chunk in range(chunks + 1):
        if chunk < chunks:
            place(chunk)
        if chunk > 0:
            convolve(chunk - 1)

    fetch.wait()
    for chunk in range(chunks):
        pair_copy(chunk).wait_recv()

    def key_copy(chunk):
        return pltpu.make_async_remote_copy(
            src_ref=keys_own.at[chunk],
            dst_ref=keys_prior.at[chunk],
            send_sem=key_send.at[chunk],
            recv_sem=key_recv.at[chunk],
            device_id={"seq": below},
            device_id_type=MESH,
        )

    def value_copy(chunk):
        return pltpu.make_async_remote_copy(
            src_ref=values_own.at[chunk],
            dst_ref=values_prior.at[chunk],
            send_sem=value_send.at[chunk],
            recv_sem=value_recv.at[chunk],
            device_id={"seq": below},
            device_id_type=MESH,
        )

    blocks = tok_dev // QUERY_ROWS

    def block_of(index):
        return pl.ds(pl.multiple_of(index * QUERY_ROWS, QUERY_ROWS), QUERY_ROWS)

    def project_keys(index, carry):
        rows = block_of(index)
        product = jnp.dot(
            mixed_ref[rows, :], weights_ref[:, local_dim:], preferred_element_type=jnp.float32
        )
        for chunk in range(chunks):
            first = chunk * LANES
            keys = jnp.transpose(product[:, first : first + LANES])
            keys_own[chunk, :, rows] = keys.astype(jnp.bfloat16)
            first = local_dim + first
            values_own[chunk, rows, :] = product[:, first : first + LANES].astype(jnp.bfloat16)
        return carry

    lax.fori_loop(0, blocks, project_keys, 0)
    for chunk in range(chunks):
        key_copy(chunk).start()
        value_copy(chunk).start()

    heads = LANES // head_dim
    lane_q = iota((QUERY_ROWS, LANES), 1) // head_dim
    lane_v = iota((tok_dev, LANES), 1) // head_dim
    log_scale = math.log2(math.e) / math.sqrt(head_dim)

    def project_queries(index, carry):
        rows = block_of(index)
        product = jnp.dot(
            mixed_ref[rows, :], weights_ref[:, :local_dim], preferred_element_type=jnp.float32
        ).astype(jnp.bfloat16)
        for chunk in range(chunks):
            query = product[:, chunk * LANES : (chunk + 1) * LANES].astype(jnp.float32) * log_scale
            coarse = query.astype(jnp.bfloat16).astype(jnp.float32)
            fine = pltpu.roll(query - coarse, head_dim, 1)
            for head in range(heads):
                queries[chunk, head, rows, :] = jnp.where(lane_q == head, coarse, fine).astype(
                    jnp.bfloat16
                )
        return carry

    lax.fori_loop(0, blocks, project_queries, 0)

    def partial(chunk, rows, keys_ref, values_ref):
        values = values_ref[chunk]
        scores = []
        for head in range(heads):
            keys = keys_ref[chunk, head * head_dim : (head + 1) * head_dim, :]
            scores.append(
                jnp.dot(
                    queries[chunk, head, rows, :],
                    jnp.concatenate([keys] * heads, axis=0),
                    preferred_element_type=jnp.float32,
                )
            )
        peaks = [jnp.max(score, axis=1, keepdims=True) for score in scores]
        pairs = []
        for head in range(heads):
            probs = jnp.exp2(scores[head] - peaks[head]).astype(jnp.bfloat16)
            pairs.append(
                jnp.dot(
                    probs,
                    jnp.where(lane_v == head, values, jnp.ones_like(values)),
                    preferred_element_type=jnp.float32,
                )
            )
        first = lane_q == 0
        peak = jnp.where(first, peaks[0], peaks[1])
        summed = jnp.where(first, pairs[0], pairs[1])
        total = pltpu.roll(jnp.where(first, pairs[1], pairs[0]), head_dim, 1)
        return peak, total, summed

    def own_chunk(chunk, carry):
        def attend_own(index, inner):
            rows = block_of(index)
            peak, total, summed = partial(chunk, rows, keys_own, values_own)
            top[chunk, rows, :] = peak
            denom[chunk, rows, :] = total
            numer[chunk, rows, :] = summed
            return inner

        return lax.fori_loop(0, blocks, attend_own, carry)

    lax.fori_loop(0, chunks, own_chunk, 0)

    def prior_chunk(chunk, carry):
        key_copy(chunk).wait_recv()
        value_copy(chunk).wait_recv()

        def attend_prior(index, inner):
            rows = block_of(index)
            peak, total, summed = partial(chunk, rows, keys_prior, values_prior)
            before = top[chunk, rows, :]
            high = jnp.maximum(peak, before)
            here = jnp.exp2(peak - high)
            there = jnp.exp2(before - high)
            total = total * here + denom[chunk, rows, :] * there
            summed = summed * here + numer[chunk, rows, :] * there
            columns = pl.ds(pl.multiple_of(chunk * LANES, LANES), LANES)
            out_ref[rows, columns] = (summed / total).astype(jnp.bfloat16)
            return inner

        return lax.fori_loop(0, blocks, attend_prior, carry)

    lax.fori_loop(0, chunks, prior_chunk, 0)

    each_peer(lambda peer: place_copy(peer, me).wait_send())
    for chunk in range(chunks):
        pair_copy(chunk).wait_send()
        if chunk + 2 >= chunks:
            each_peer(lambda peer: token_copy(chunk, peer, me).wait_send())

        @pl.when(has_above)
        def _():
            copy_up(chunk).wait_send()

        @pl.when(has_below)
        def _():
            copy_down(chunk).wait_send()

    for chunk in range(chunks):
        key_copy(chunk).wait_send()
        value_copy(chunk).wait_send()


def shards(features, cells, conv7, conv5, conv3, conv_bias, w_qkv):
    tok_dev, local_dim = features.shape
    members = lax.axis_size("seq")
    capacity = 2 * tok_dev // members
    chunks = local_dim // LANES
    head_dim = D // HEADS
    band_rows = tok_dev // GRID_W
    halo_len = HALO * GRID_W
    vmem = pl.BlockSpec(memory_space=pltpu.VMEM)
    dma = pltpu.SemaphoreType.DMA

    merged = conv7.astype(jnp.float32) + jnp.pad(
        conv5.astype(jnp.float32), ((1, 1), (1, 1), (0, 0))
    )
    merged = merged + jnp.pad(conv3.astype(jnp.float32), ((2, 2), (2, 2), (0, 0)))
    merged = merged + jnp.pad(jnp.ones((1, 1, local_dim), jnp.float32), ((3, 3), (3, 3), (0, 0)))
    taps = merged.reshape(REACH * REACH, local_dim)
    bias = conv_bias.astype(jnp.float32).reshape(1, local_dim)

    weights = w_qkv.reshape(w_qkv.shape[0], 3 * local_dim)
    half_words = functools.partial(pltpu.VMEM, dtype=jnp.bfloat16)
    words = functools.partial(pltpu.VMEM, dtype=jnp.float32)
    return pl.pallas_call(
        functools.partial(band_kernel, members, head_dim),
        out_shape=jax.ShapeDtypeStruct((tok_dev, local_dim), jnp.bfloat16),
        in_specs=[vmem, vmem, pl.BlockSpec(memory_space=pl.ANY), vmem, vmem],
        out_specs=vmem,
        scratch_shapes=[
            half_words((chunks, members, capacity, LANES)),
            pltpu.VMEM((members, 8, capacity), jnp.int32),
            half_words((tok_dev, 2 * local_dim)),
            half_words((chunks, members, capacity, LANES)),
            pltpu.VMEM((members, 8, capacity), jnp.int32),
            half_words((tok_dev, members * capacity)),
            half_words((chunks, tok_dev, LANES)),
            half_words((chunks, halo_len, LANES)),
            half_words((chunks, halo_len, LANES)),
            words((band_rows + 2 * HALO, GRID_W + 2 * PAD, LANES)),
            half_words(weights.shape),
            half_words((chunks, LANES // head_dim, tok_dev, LANES)),
            half_words((chunks, LANES, tok_dev)),
            half_words((chunks, tok_dev, LANES)),
            half_words((chunks, LANES, tok_dev)),
            half_words((chunks, tok_dev, LANES)),
            words((chunks, tok_dev, LANES)),
            words((chunks, tok_dev, LANES)),
            words((chunks, tok_dev, LANES)),
            dma,
            dma((chunks, members)),
            dma((chunks, members)),
            dma((members,)),
            dma((members,)),
        ]
        + [dma((chunks,))] * 10,
        compiler_params=pltpu.CompilerParams(
            collective_id=0, has_side_effects=True, vmem_limit_bytes=VMEM_BYTES
        ),
        name="band",
    )(cells.reshape(1, tok_dev), features, weights, taps, bias)


def solution(mesh):
    placed = (
        P("seq", "head"),
        P("seq"),
        P(None, None, "head"),
        P(None, None, "head"),
        P(None, None, "head"),
        P("head"),
        P(None, None, "head"),
    )
    return jax.shard_map(
        shards, mesh=mesh, in_specs=placed, out_specs=P("seq", "head"), check_vma=False
    )
```

```python
import functools
import math

import jax
import jax.numpy as jnp
from jax import lax
from jax.experimental import pallas as pl
from jax.experimental.pallas import tpu as pltpu
from jax.sharding import PartitionSpec as P

D = 1024
HEADS = 16
GRID_W = 256
LANES = 128
PAD = 8
STRIP = 32
REACH = 7
HALO = REACH // 2
QUERY_ROWS = 512
MESH = pl.DeviceIdType.MESH
VMEM_BYTES = 56 * 1024 * 1024


def iota(shape, dim):
    return lax.broadcasted_iota(jnp.int32, shape, dim)


def flags(condition):
    return jnp.where(condition, 1.0, 0.0)


def band_kernel(
    members,
    head_dim,
    cells_ref,
    features_ref,
    weights_hbm,
    taps_ref,
    bias_ref,
    out_ref,
    outgoing_ref,
    places_ref,
    mixed_ref,
    arrived,
    places_in,
    gather,
    band_bf16,
    halo_up,
    halo_down,
    padded,
    weights_ref,
    queries,
    keys_own,
    values_own,
    keys_prior,
    values_prior,
    top,
    numer,
    denom,
    weight_sem,
    out_send,
    out_recv,
    place_send,
    place_recv,
    up_send,
    up_recv,
    down_send,
    down_recv,
    pair_send,
    pair_recv,
    key_send,
    key_recv,
    value_send,
    value_recv,
):
    chunks, _, capacity, _ = outgoing_ref.shape
    fetches = [
        pltpu.make_async_copy(weights_hbm.at[kind], weights_ref.at[kind], weight_sem.at[kind])
        for kind in range(3)
    ]
    for fetch in fetches:
        fetch.start()
    tok_dev, local_dim = out_ref.shape
    band_rows = tok_dev // GRID_W
    halo_len = HALO * GRID_W
    me = lax.axis_index("seq")
    half = lax.axis_index("head")

    barrier = pltpu.get_barrier_semaphore()

    def greet(step, carry):
        peer = lax.rem(me + step, members)
        pl.semaphore_signal(barrier, inc=1, device_id={"seq": peer}, device_id_type=MESH)
        return carry

    lax.fori_loop(1, members, greet, 0)
    pl.semaphore_signal(barrier, inc=1, device_id={"head": 1 - half}, device_id_type=MESH)
    pl.semaphore_wait(barrier, members)

    def place_copy(peer, slot):
        return pltpu.make_async_remote_copy(
            src_ref=places_ref.at[peer],
            dst_ref=places_in.at[slot],
            send_sem=place_send.at[peer],
            recv_sem=place_recv.at[slot],
            device_id={"seq": peer},
            device_id_type=MESH,
        )

    def token_copy(chunk, peer, slot):
        return pltpu.make_async_remote_copy(
            src_ref=outgoing_ref.at[chunk, peer],
            dst_ref=arrived.at[chunk, slot],
            send_sem=out_send.at[chunk, peer],
            recv_sem=out_recv.at[chunk, slot],
            device_id={"seq": peer},
            device_id_type=MESH,
        )

    def each_peer(action):
        def step_body(step, carry):
            away = (step + 1) // 2
            shift = members // 2 + lax.select(lax.rem(step, 2) == 1, away, -away)
            action(lax.rem(me + shift, members))
            return carry

        lax.fori_loop(0, members - 1, step_body, 0)

    cells = cells_ref[...]
    owner = ((cells.astype(jnp.float32) + 0.5) * (1.0 / tok_dev)).astype(jnp.int32)
    within = cells - owner * tok_dev
    onehot = flags(iota((members, tok_dev), 0) == owner)
    upper = flags(iota((tok_dev, tok_dev), 0) < iota((tok_dev, tok_dev), 1))
    earlier = jnp.dot(
        onehot.astype(jnp.bfloat16),
        upper.astype(jnp.bfloat16),
        preferred_element_type=jnp.float32,
    )
    rank = jnp.sum(earlier * onehot, axis=0, keepdims=True)
    slot = owner * capacity + rank.astype(jnp.int32)
    line = iota((8, tok_dev), 0)
    high = (within >> 8).astype(jnp.float32)
    low = (within & 255).astype(jnp.float32)
    code = jnp.where(line == 0, high, jnp.where(line == 1, low, jnp.where(line == 2, 1.0, 0.0)))
    code = code.astype(jnp.bfloat16)

    def pack(band):
        pick = flags(iota((capacity, tok_dev), 0) + band * capacity == slot).astype(jnp.bfloat16)
        rows = jnp.dot(pick, features_ref[...], preferred_element_type=jnp.float32)
        rows = rows.astype(jnp.bfloat16)
        for chunk in range(chunks):
            outgoing_ref[chunk, band] = rows[:, chunk * LANES : (chunk + 1) * LANES]
        found = lax.dot_general(
            code, pick, (((1,), (1,)), ((), ())), preferred_element_type=jnp.float32
        )
        spot = jnp.where(found[2:3] > 0.5, found[0:1] * 256.0 + found[1:2], -1.0)
        places_ref[band] = jnp.broadcast_to(spot.astype(jnp.int32), (8, capacity))

    def pack_and_send(peer):
        pack(peer)
        place_copy(peer, me).start()
        token_copy(0, peer, me).start()

    each_peer(pack_and_send)
    if chunks > 1:
        each_peer(lambda peer: token_copy(1, peer, me).start())
    pack(me)

    places_in[pl.ds(me, 1)] = places_ref[pl.ds(me, 1)]
    for chunk in range(chunks):
        arrived[chunk, pl.ds(me, 1)] = outgoing_ref[chunk, pl.ds(me, 1)]
    edge = jnp.zeros((band_rows + 2 * HALO, PAD, LANES), jnp.float32)
    padded[:, 0:PAD, :] = edge
    padded[:, PAD + GRID_W :, :] = edge

    each_peer(lambda peer: place_copy(peer, peer).wait_recv())

    def pick_rows(row, carry):
        start = pl.multiple_of(row * GRID_W, GRID_W)
        cell = iota((GRID_W, capacity), 0) + start
        for source in range(members):
            hit = flags(cell == places_in[source, 0:1, :])
            gather[pl.ds(start, GRID_W), source * capacity : (source + 1) * capacity] = hit.astype(
                jnp.bfloat16
            )
        return carry

    lax.fori_loop(0, band_rows, pick_rows, 0)

    above = lax.rem(me + members - 1, members)
    below = lax.rem(me + 1, members)

    def copy_up(chunk):
        return pltpu.make_async_remote_copy(
            src_ref=band_bf16.at[chunk, pl.ds(0, halo_len)],
            dst_ref=halo_down.at[chunk],
            send_sem=up_send.at[chunk],
            recv_sem=up_recv.at[chunk],
            device_id={"seq": above},
            device_id_type=MESH,
        )

    def copy_down(chunk):
        return pltpu.make_async_remote_copy(
            src_ref=band_bf16.at[chunk, pl.ds(tok_dev - halo_len, halo_len)],
            dst_ref=halo_up.at[chunk],
            send_sem=down_send.at[chunk],
            recv_sem=down_recv.at[chunk],
            device_id={"seq": below},
            device_id_type=MESH,
        )

    def own_columns(chunk):
        return pl.ds(pl.multiple_of(half * local_dim + chunk * LANES, LANES), LANES)

    def pair_copy(chunk):
        return pltpu.make_async_remote_copy(
            src_ref=mixed_ref.at[:, own_columns(chunk)],
            dst_ref=mixed_ref.at[:, own_columns(chunk)],
            send_sem=pair_send.at[chunk],
            recv_sem=pair_recv.at[chunk],
            device_id={"head": 1 - half},
            device_id_type=MESH,
        )

    has_above = me > 0
    has_below = me < members - 1

    def place(chunk):
        each_peer(lambda peer: token_copy(chunk, peer, peer).wait_recv())
        tokens = arrived[chunk].reshape(members * capacity, LANES)
        for row in range(band_rows):
            cells = slice(row * GRID_W, (row + 1) * GRID_W)
            found = jnp.dot(gather[cells, :], tokens, preferred_element_type=jnp.float32)
            band_bf16[chunk, cells, :] = found.astype(jnp.bfloat16)

        @pl.when(has_above)
        def _():
            copy_up(chunk).start()

        @pl.when(has_below)
        def _():
            copy_down(chunk).start()

        if chunk + 2 < chunks:
            each_peer(lambda peer: token_copy(chunk, peer, me).wait_send())
            each_peer(lambda peer: token_copy(chunk + 2, peer, me).start())

    def convolve(chunk):
        for row in range(band_rows):
            padded[HALO + row, PAD : PAD + GRID_W, :] = band_bf16[
                chunk, row * GRID_W : (row + 1) * GRID_W, :
            ].astype(jnp.float32)

        blank = jnp.zeros((HALO, GRID_W, LANES), jnp.float32)

        @pl.when(has_above)
        def _():
            copy_down(chunk).wait_recv()
            for row in range(HALO):
                padded[row, PAD : PAD + GRID_W, :] = halo_up[
                    chunk, row * GRID_W : (row + 1) * GRID_W, :
                ].astype(jnp.float32)

        @pl.when(jnp.logical_not(has_above))
        def _():
            padded[0:HALO, PAD : PAD + GRID_W, :] = blank

        @pl.when(has_below)
        def _():
            copy_up(chunk).wait_recv()
            for row in range(HALO):
                padded[HALO + band_rows + row, PAD : PAD + GRID_W, :] = halo_down[
                    chunk, row * GRID_W : (row + 1) * GRID_W, :
                ].astype(jnp.float32)

        @pl.when(jnp.logical_not(has_below))
        def _():
            padded[HALO + band_rows :, PAD : PAD + GRID_W, :] = blank

        lanes = slice(chunk * LANES, (chunk + 1) * LANES)
        columns = own_columns(chunk)

        def strip(index, carry):
            start = pl.multiple_of(index * STRIP, STRIP)
            sums = [jnp.broadcast_to(bias_ref[:, lanes], (STRIP, LANES))] * band_rows
            for j in range(REACH):
                taps = [taps_ref[i * REACH + j : i * REACH + j + 1, lanes] for i in range(REACH)]
                for line in range(band_rows + 2 * HALO):
                    cells = padded[line, pl.ds(start + (PAD - HALO + j), STRIP), :]
                    for row in range(max(0, line - 2 * HALO), min(band_rows, line + 1)):
                        sums[row] = sums[row] + cells * taps[line - row]
            for row in range(band_rows):
                value = sums[row].astype(jnp.bfloat16)
                where = pl.ds(pl.multiple_of(row * GRID_W + start, STRIP), STRIP)
                mixed_ref[where, columns] = value
            return carry

        lax.fori_loop(0, GRID_W // STRIP, strip, 0)
        pair_copy(chunk).start()

    for chunk in range(chunks + 1):
        if chunk < chunks:
            place(chunk)
        if chunk > 0:
            convolve(chunk - 1)

    for fetch in fetches:
        fetch.wait()
    for chunk in range(chunks):
        pair_copy(chunk).wait_recv()

    def key_copy(chunk):
        return pltpu.make_async_remote_copy(
            src_ref=keys_own.at[chunk],
            dst_ref=keys_prior.at[chunk],
            send_sem=key_send.at[chunk],
            recv_sem=key_recv.at[chunk],
            device_id={"seq": below},
            device_id_type=MESH,
        )

    def value_copy(chunk):
        return pltpu.make_async_remote_copy(
            src_ref=values_own.at[chunk],
            dst_ref=values_prior.at[chunk],
            send_sem=value_send.at[chunk],
            recv_sem=value_recv.at[chunk],
            device_id={"seq": below},
            device_id_type=MESH,
        )

    blocks = tok_dev // QUERY_ROWS

    def block_of(index):
        return pl.ds(pl.multiple_of(index * QUERY_ROWS, QUERY_ROWS), QUERY_ROWS)

    def project_keys(index, carry):
        rows = block_of(index)
        key_rows, value_rows = (
            jnp.dot(mixed_ref[rows, :], weights_ref[kind], preferred_element_type=jnp.float32)
            for kind in (1, 2)
        )
        for chunk in range(chunks):
            columns = slice(chunk * LANES, (chunk + 1) * LANES)
            keys_own[chunk, :, rows] = jnp.transpose(key_rows[:, columns]).astype(jnp.bfloat16)
            values_own[chunk, rows, :] = value_rows[:, columns].astype(jnp.bfloat16)
        return carry

    lax.fori_loop(0, blocks, project_keys, 0)
    for chunk in range(chunks):
        key_copy(chunk).start()
        value_copy(chunk).start()

    heads = LANES // head_dim
    lane_q = iota((QUERY_ROWS, LANES), 1) // head_dim
    lane_v = iota((tok_dev, LANES), 1) // head_dim
    log_scale = math.log2(math.e) / math.sqrt(head_dim)

    def project_queries(index, carry):
        rows = block_of(index)
        product = jnp.dot(
            mixed_ref[rows, :], weights_ref[0], preferred_element_type=jnp.float32
        ).astype(jnp.bfloat16)
        for chunk in range(chunks):
            query = product[:, chunk * LANES : (chunk + 1) * LANES].astype(jnp.float32) * log_scale
            coarse = query.astype(jnp.bfloat16).astype(jnp.float32)
            fine = pltpu.roll(query - coarse, head_dim, 1)
            for head in range(heads):
                queries[chunk, head, rows, :] = jnp.where(lane_q == head, coarse, fine).astype(
                    jnp.bfloat16
                )
        return carry

    lax.fori_loop(0, blocks, project_queries, 0)

    def partial(chunk, rows, keys_ref, values_ref):
        values = values_ref[chunk]
        scores = []
        for head in range(heads):
            keys = keys_ref[chunk, head * head_dim : (head + 1) * head_dim, :]
            scores.append(
                jnp.dot(
                    queries[chunk, head, rows, :],
                    jnp.concatenate([keys] * heads, axis=0),
                    preferred_element_type=jnp.float32,
                )
            )
        peaks = [jnp.max(score, axis=1, keepdims=True) for score in scores]
        pairs = []
        for head in range(heads):
            probs = jnp.exp2(scores[head] - peaks[head]).astype(jnp.bfloat16)
            pairs.append(
                jnp.dot(
                    probs,
                    jnp.where(lane_v == head, values, jnp.ones_like(values)),
                    preferred_element_type=jnp.float32,
                )
            )
        first = lane_q == 0
        peak = jnp.where(first, peaks[0], peaks[1])
        summed = jnp.where(first, pairs[0], pairs[1])
        total = pltpu.roll(jnp.where(first, pairs[1], pairs[0]), head_dim, 1)
        return peak, total, summed

    def own_chunk(chunk, carry):
        def attend_own(index, inner):
            rows = block_of(index)
            peak, total, summed = partial(chunk, rows, keys_own, values_own)
            top[chunk, rows, :] = peak
            denom[chunk, rows, :] = total
            numer[chunk, rows, :] = summed
            return inner

        return lax.fori_loop(0, blocks, attend_own, carry)

    lax.fori_loop(0, chunks, own_chunk, 0)

    def prior_chunk(chunk, carry):
        key_copy(chunk).wait_recv()
        value_copy(chunk).wait_recv()

        def attend_prior(index, inner):
            rows = block_of(index)
            peak, total, summed = partial(chunk, rows, keys_prior, values_prior)
            before = top[chunk, rows, :]
            high = jnp.maximum(peak, before)
            here = jnp.exp2(peak - high)
            there = jnp.exp2(before - high)
            total = total * here + denom[chunk, rows, :] * there
            summed = summed * here + numer[chunk, rows, :] * there
            columns = pl.ds(pl.multiple_of(chunk * LANES, LANES), LANES)
            out_ref[rows, columns] = (summed / total).astype(jnp.bfloat16)
            return inner

        return lax.fori_loop(0, blocks, attend_prior, carry)

    lax.fori_loop(0, chunks, prior_chunk, 0)

    each_peer(lambda peer: place_copy(peer, me).wait_send())
    for chunk in range(chunks):
        pair_copy(chunk).wait_send()
        if chunk + 2 >= chunks:
            each_peer(lambda peer: token_copy(chunk, peer, me).wait_send())

        @pl.when(has_above)
        def _():
            copy_up(chunk).wait_send()

        @pl.when(has_below)
        def _():
            copy_down(chunk).wait_send()

    for chunk in range(chunks):
        key_copy(chunk).wait_send()
        value_copy(chunk).wait_send()


def shards(features, cells, conv7, conv5, conv3, conv_bias, w_qkv):
    tok_dev, local_dim = features.shape
    members = lax.axis_size("seq")
    capacity = 2 * tok_dev // members
    chunks = local_dim // LANES
    head_dim = D // HEADS
    band_rows = tok_dev // GRID_W
    halo_len = HALO * GRID_W
    vmem = pl.BlockSpec(memory_space=pltpu.VMEM)
    dma = pltpu.SemaphoreType.DMA

    merged = conv7.astype(jnp.float32) + jnp.pad(
        conv5.astype(jnp.float32), ((1, 1), (1, 1), (0, 0))
    )
    merged = merged + jnp.pad(conv3.astype(jnp.float32), ((2, 2), (2, 2), (0, 0)))
    merged = merged + jnp.pad(jnp.ones((1, 1, local_dim), jnp.float32), ((3, 3), (3, 3), (0, 0)))
    taps = merged.reshape(REACH * REACH, local_dim)
    bias = conv_bias.astype(jnp.float32).reshape(1, local_dim)

    weights = jnp.transpose(w_qkv, (1, 0, 2))
    half_words = functools.partial(pltpu.VMEM, dtype=jnp.bfloat16)
    words = functools.partial(pltpu.VMEM, dtype=jnp.float32)
    return pl.pallas_call(
        functools.partial(band_kernel, members, head_dim),
        out_shape=jax.ShapeDtypeStruct((tok_dev, local_dim), jnp.bfloat16),
        in_specs=[vmem, vmem, pl.BlockSpec(memory_space=pl.ANY), vmem, vmem],
        out_specs=vmem,
        scratch_shapes=[
            half_words((chunks, members, capacity, LANES)),
            pltpu.VMEM((members, 8, capacity), jnp.int32),
            half_words((tok_dev, 2 * local_dim)),
            half_words((chunks, members, capacity, LANES)),
            pltpu.VMEM((members, 8, capacity), jnp.int32),
            half_words((tok_dev, members * capacity)),
            half_words((chunks, tok_dev, LANES)),
            half_words((chunks, halo_len, LANES)),
            half_words((chunks, halo_len, LANES)),
            words((band_rows + 2 * HALO, GRID_W + 2 * PAD, LANES)),
            half_words((3, 2 * local_dim, local_dim)),
            half_words((chunks, LANES // head_dim, tok_dev, LANES)),
            half_words((chunks, LANES, tok_dev)),
            half_words((chunks, tok_dev, LANES)),
            half_words((chunks, LANES, tok_dev)),
            half_words((chunks, tok_dev, LANES)),
            words((chunks, tok_dev, LANES)),
            words((chunks, tok_dev, LANES)),
            words((chunks, tok_dev, LANES)),
            dma((3,)),
            dma((chunks, members)),
            dma((chunks, members)),
            dma((members,)),
            dma((members,)),
        ]
        + [dma((chunks,))] * 10,
        compiler_params=pltpu.CompilerParams(
            collective_id=0, has_side_effects=True, vmem_limit_bytes=VMEM_BYTES
        ),
        name="band",
    )(cells.reshape(1, tok_dev), features, weights, taps, bias)


def solution(mesh):
    placed = (
        P("seq", "head"),
        P("seq"),
        P(None, None, "head"),
        P(None, None, "head"),
        P(None, None, "head"),
        P("head"),
        P(None, None, "head"),
    )
    return jax.shard_map(
        shards, mesh=mesh, in_specs=placed, out_specs=P("seq", "head"), check_vma=False
    )
```
